128 devices in a mesh: ka: 16 (over z_lo, x, core), ga: 8 (over y, z_hi).
Axes of the slice: x: 4, y: 4, z: 4 (z_hi: 2, z_lo: 2; z = z_hi * 2 + z_lo), core: 2. Of those that a mesh axis runs over, the one named last changes fastest.
Arguments:
- diag_waves: float32 [16, 8, 2, 4096], P('ka'), may hold values from -6 to 6
- band_waves: float32 [16, 72, 2, 4096], P('ka', 'ga'), may hold values from -6 to 6
- screening: float32 [2, 2, 4096, 4096], P(None, None, 'ga', 'ka'), may hold values from -0.09375 to 0.09375
- partner_map: int32 [2, 16], replicated, may hold values from 0 to 15, as said below
- grid_index: int32 [4096], replicated, may hold values from 0 to 4095, each once
Outputs:
- self_energy: float32 [2, 16, 8], P(None, 'ka')
The draws below stay inside these ranges and needn't reach their ends.
Inputs may be any that keep to these rules, and one draw needn't show every extreme that they name: For each q-step q there is one shift s_q: partner_map[q, k] lies in the block of 1 consecutive k-points with block number (k - s_q) mod (16), and partner_map[q] is a permutation of the k-points; one q-step has s_q = 1 and the other s_q = 8, in either order. `grid_index`: a permutation of the flattened grid points g1 * 64 + g2.
All inputs are finite; a program needn't handle non-finite values.
Results may differ from the reference program's by a relative error of at most 0.0056.
Values may be sent and summed in bfloat16 or wider, within the bound.
No kernel may reach another device: no remote copies, remote signals or barrier semaphores. Data moves between devices by JAX's collectives and lax.ppermute only.
A program may use at most 256 MiB of HBM per device.

```python
import math
import jax
import jax.numpy as jnp
from jax import lax

N1 = 64
N2 = 64
NR = 4096
NG = 4096
NBD = 8
MB = 72
QSTEPS = 2
K_DEV = 1
KPTS = 16


def inner_order(one_key):
    return jax.random.permutation(one_key, K_DEV)


def draw_partner_map(key, part):
    key = jax.random.fold_in(key, 7)
    shift_key, inner_key = jax.random.split(key)
    blocks = KPTS // K_DEV
    first = jax.random.randint(shift_key, (), 0, 2).astype(jnp.int32)
    steps = jnp.arange(QSTEPS, dtype=jnp.int32)
    shifts = jnp.where(steps == first, 1, max(blocks // 2, 1)).astype(jnp.int32)
    inner = jax.vmap(inner_order)(jax.random.split(inner_key, QSTEPS * blocks))
    inner = inner.reshape(QSTEPS, KPTS).astype(jnp.int32)
    points = jnp.arange(KPTS, dtype=jnp.int32)
    source = (points[None, :] // K_DEV - shifts[:, None]) % blocks
    return (source * K_DEV + inner).astype(jnp.int32)


def block_levels(own_key, shape, pieces, low, high):
    def one(position, blocks):
        steps = jax.random.uniform(jax.random.fold_in(jax.random.fold_in(own_key, 6), position), (blocks,), jnp.float32, low / len(pieces), high / len(pieces))
        return jnp.repeat(jnp.exp(steps), shape[position] // blocks).reshape((-1,) + (1,) * (len(shape) - position - 1))

    level = one(*pieces[0])
    for cut in pieces[1:]:
        level = level * one(*cut)
    return level


def normal_values(stream_key, extent, width, limit, shards=(), kind=jnp.bfloat16):
    drawn = width * jax.random.normal(stream_key, extent, jnp.float32)
    if shards:
        drawn = drawn * block_levels(stream_key, extent, shards, -0.22, 0.18)
    return jnp.clip(drawn, -limit, limit).astype(kind)


def setup_inputs(seed: int = 0) -> dict:
    arg_keys = jax.random.split(jax.random.key(seed), 6)
    return {
        "diag_waves": normal_values(arg_keys[0], (KPTS, NBD, 2, NR), 1.0, 6.0, ((0, 16),), jnp.float32),
        "band_waves": normal_values(arg_keys[1], (KPTS, MB, 2, NR), 1.0, 6.0, ((0, 16), (1, 8)), jnp.float32),
        "screening": normal_values(arg_keys[2], (QSTEPS, 2, NG, NG), NG ** -0.5, 0.09375, ((2, 8), (3, 16)), jnp.float32),
        "partner_map": draw_partner_map(jax.random.fold_in(arg_keys[5], 71), 0),
        "grid_index": jax.random.permutation(arg_keys[4], NG).astype(jnp.int32),
    }


def pair_block(diag_point, band_point, grid_index):
    diag_re = diag_point[:, 0][:, None, :]
    diag_im = diag_point[:, 1][:, None, :]
    band_re = band_point[:, 0][None, :, :]
    band_im = band_point[:, 1][None, :, :]
    rho_re = diag_re * band_re + diag_im * band_im
    rho_im = diag_re * band_im - diag_im * band_re
    field = lax.complex(rho_re, rho_im).reshape(NBD, MB, N1, N2)
    spectrum = jnp.fft.fft2(field).reshape(NBD, MB, NR) / math.sqrt(NR)
    picked = jnp.take(spectrum, grid_index, axis=2)
    pair_re = jnp.real(picked).astype(jnp.bfloat16).reshape(NBD * MB, NG)
    pair_im = jnp.imag(picked).astype(jnp.bfloat16).reshape(NBD * MB, NG)
    return (pair_re, pair_im)

def reference(diag_waves, band_waves, screening, partner_map, grid_index):
    total = jnp.zeros((2, KPTS, NBD), jnp.float32)
    for qstep in range(QSTEPS):
        screen_half = screening[qstep].astype(jnp.bfloat16)
        screen_re = screen_half[0].T
        screen_im = screen_half[1].T

        def one_point(kpoint):
            partner = partner_map[qstep, kpoint]
            diag_point = lax.dynamic_index_in_dim(diag_waves, kpoint, 0, keepdims=False)
            band_point = lax.dynamic_index_in_dim(band_waves, partner, 0, keepdims=False)
            pair_re, pair_im = pair_block(diag_point, band_point, grid_index)
            image_re = jnp.dot(pair_re, screen_re, preferred_element_type=jnp.float32) - jnp.dot(pair_im, screen_im, preferred_element_type=jnp.float32)
            image_im = jnp.dot(pair_re, screen_im, preferred_element_type=jnp.float32) + jnp.dot(pair_im, screen_re, preferred_element_type=jnp.float32)
            left_re = pair_re.astype(jnp.float32)
            left_im = pair_im.astype(jnp.float32)
            sum_re = lax.optimization_barrier(jnp.sum((left_re * image_re + left_im * image_im).reshape(NBD, MB * NG), axis=1))
            sum_im = lax.optimization_barrier(jnp.sum((left_re * image_im - left_im * image_re).reshape(NBD, MB * NG), axis=1))
            return jnp.stack([sum_re, sum_im])
        values = lax.map(one_point, jnp.arange(KPTS, dtype=jnp.int32))
        total = total + jnp.transpose(values, (1, 0, 2))
    return total * (-1.0 / (QSTEPS * MB * math.sqrt(NG)))
```

```python
import math

import jax
import jax.numpy as jnp
import numpy as np
from jax import lax
from jax.experimental import pallas as pl
from jax.experimental.pallas import tpu as pltpu
from jax.sharding import PartitionSpec as P

N1 = 64
NG = 4096
MB = 72
NBD = 8
QSTEPS = 2
KA = 16
GA = 8
F32 = jnp.float32
BF16 = jnp.bfloat16
VMEM_BYTES = 48 * 1024 * 1024
ALL = ("ka", "ga")


def split_table(table):
    high = table.astype(jnp.bfloat16)
    low = (table - high.astype(np.float64)).astype(jnp.bfloat16)
    return high, low


def make_tables():
    places = np.arange(N1)
    angle = (places[:, None] * places[None, :] % N1) * (2.0 * math.pi / N1)
    cos, sin = np.cos(angle), np.sin(angle)
    high, low = split_table(np.concatenate([cos, sin], 0))
    exact_in = np.concatenate([high, low], 1)
    split_in = np.concatenate([high, high, low], 1)
    wide = np.concatenate([cos, sin], 1)
    block = np.zeros((2 * N1, 4 * N1))
    block[:N1, : 2 * N1] = wide
    block[N1:, 2 * N1 :] = wide
    high, low = split_table(block)
    turned = np.concatenate([high, high, low], 0)
    return exact_in, split_in, turned


def lane_sign(rows, first):
    lane = lax.broadcasted_iota(jnp.int32, (rows, 128), 1)
    return jnp.where(lane < 64, first, -first).astype(F32)


def swap_halves(x):
    return pltpu.roll(x, 64, 1)


def split_rows(x):
    high = x.astype(BF16)
    low = (x - high.astype(F32)).astype(BF16)
    return high, low


def dot(a, b):
    return jnp.dot(a, b, preferred_element_type=F32)


def pack_kernel(w_ref, extra_ref, out_ref):
    lane = lax.broadcasted_iota(jnp.int32, (512, 128), 1) // 32
    for dest in range(GA):
        half, place = dest // 4, dest % 4
        total = None
        for slot in range(4):
            part, qstep = slot // 2, slot % 2
            source = w_ref[qstep, part, :, half * 128 : (half + 1) * 128]
            shift = (slot - place) * 32 % 128
            moved = pltpu.roll(source, shift, 1) if shift else source
            total = moved if total is None else jnp.where(lane == slot, moved, total)
        out_ref[dest, 0:512, :] = total.astype(BF16)
        out_ref[dest, 512:592, :] = extra_ref[dest]


def scatter_rows(place_ref, from_ref, to_ref):
    def step(block, carry):
        for inner in range(64):
            row = block * 64 + inner
            to_ref[pl.ds(place_ref[row], 1), :] = from_ref[pl.ds(row, 1), :]
        return carry

    lax.fori_loop(0, NG // 64, step, 0)


def first_axis(exact_ref, grid_ref, half_ref, sign):
    table = exact_ref[...]
    signs = lane_sign(64, sign)

    def step(pair, carry):
        rows = grid_ref[pl.ds(pl.multiple_of(pair * 128, 128), 128), :].astype(BF16)
        left, right = rows[:64], rows[64:]
        stacked = jnp.concatenate(
            [jnp.concatenate([left, left], 0), jnp.concatenate([right, right], 0)], 1
        )
        out = dot(table, stacked)
        for side in range(2):
            piece = out[:, side * 128 : (side + 1) * 128]
            mixed = piece[:64] + signs * swap_halves(piece[64:])
            half_ref[pl.ds(pl.multiple_of(pair * 128 + side * 64, 64), 64), :] = mixed
        return carry

    lax.fori_loop(0, 32, step, 0, unroll=16)


def rows_kernel(place_ref, got_ref, extra_ref, exact_ref, turned_ref, out_ref, waves_ref, flat_ref, grid_ref, half_ref, waves_f32):
    for source in range(GA):
        flat_ref[source * 512 : (source + 1) * 512, :] = got_ref[source, 0:512, :].astype(F32)
        extra = got_ref[source, 512:592, :].astype(F32)
        for part in range(2):
            for group in range(4):
                first = (part * 4 + group) * 9
                waves_f32[part * 72 + source * 9 : part * 72 + source * 9 + 9, group * 128 : (group + 1) * 128] = extra[first : first + 9]
    waves_ref[...] = waves_f32[...].astype(BF16)
    scatter_rows(place_ref, flat_ref, grid_ref)
    first_axis(exact_ref, grid_ref, half_ref, -1.0)
    signs = lane_sign(64, -1.0)
    table = turned_ref[...]

    def step(pair, carry):
        both = jnp.concatenate(
            [half_ref[pl.ds(pair * 2 + side, 64, stride=64), :] for side in range(2)], 0
        )
        high, low = split_rows(both.T)
        out = dot(jnp.concatenate([high, low, high], 1), table)
        for side in range(2):
            piece = out[:, side * 128 : (side + 1) * 128]
            mixed = (piece[:64] + signs * swap_halves(piece[64:])).astype(BF16)
            first = pair * 2 + side
            for qstep in range(2):
                dest = (qstep * 8 + first % 8) * GA + first // 8
                out_ref[dest, 0:32, :] = mixed[qstep * 32 : (qstep + 1) * 32]
        return carry

    lax.fori_loop(0, 32, step, 0, unroll=16)

    def fill(dest, carry):
        out_ref[dest, 32:80, :] = extra_ref[dest // GA]
        return carry

    lax.fori_loop(0, KA * GA, fill, 0, unroll=16)


def columns_kernel(place_ref, got_ref, exact_ref, split_ref, out_ref, waves_ref, diag_ref, flat_ref, grid_ref, half_ref, waves_f32):
    def unpack(point, carry):
        for source in range(GA):
            index = point * GA + source
            flat_ref[pl.ds(pl.multiple_of(index * 32, 32), 32), :] = got_ref[index, 0:32, :].astype(F32)
            extra = got_ref[index, 32:80, :].astype(F32)
            for part in range(2):
                for group in range(2):
                    first = (part * 2 + group) * 9
                    lanes = slice(group * 128, (group + 1) * 128)
                    waves_f32[part * 72 + source * 9 : part * 72 + source * 9 + 9, lanes] = extra[first : first + 9]
                    row = 36 + part * 2 + group
                    diag_ref[point, part * 8 + source : part * 8 + source + 1, lanes] = (
                        extra[row : row + 1] + extra[row + 4 : row + 5]
                    )
        waves_ref[point] = waves_f32[...].astype(BF16)
        return carry

    lax.fori_loop(0, KA, unpack, 0, unroll=2)
    scatter_rows(place_ref, flat_ref, grid_ref)
    first_axis(exact_ref, grid_ref, half_ref, 1.0)
    signs = lane_sign(64, 1.0)
    table = split_ref[...]

    def step(pair, carry):
        columns = []
        for side in range(2):
            high, low = split_rows(half_ref[pl.ds(pair * 2 + side, 64, stride=64), :])
            columns.append(jnp.concatenate([high, low, high], 0))
        out = dot(table, jnp.concatenate(columns, 1))
        for side in range(2):
            piece = out[:, side * 128 : (side + 1) * 128]
            mixed = piece[:64] + signs * swap_halves(piece[64:])
            out_ref[pl.ds(pl.multiple_of(pair * 128 + side * 64, 64), 64), :] = mixed.astype(BF16)
        return carry

    lax.fori_loop(0, 32, step, 0, unroll=16)


def contract_kernel(point_ref, screen_ref, row_ref, waves_ref, diag_ref, out_ref, tile_ref):
    lane = lax.broadcasted_iota(jnp.int32, (256, 128), 1) < 64
    for qstep in range(2):
        for group in range(4):
            even = screen_ref[qstep * 8 + group * 2].astype(F32)
            odd = screen_ref[qstep * 8 + group * 2 + 1].astype(F32)
            lanes = slice(group % 2 * 128, (group % 2 + 1) * 128)
            tile_ref[qstep, 0, group // 2, :, lanes] = jnp.where(lane, even, swap_halves(odd))
            tile_ref[qstep, 1, group // 2, :, lanes] = jnp.where(lane, swap_halves(even), odd)
    out_ref[...] = jnp.zeros_like(out_ref)

    def step(partner, carry):
        near = waves_ref[partner].astype(F32)
        turned = jnp.concatenate([near, jnp.concatenate([near[72:], -near[:72]], 0)], 1).T
        turned = turned.astype(BF16)
        points = [point_ref[qstep, partner] for qstep in range(2)]
        lefts = []
        for point in points:
            diag = diag_ref[point]
            diag_re, diag_im = diag[:8], diag[8:]
            both = jnp.concatenate(
                [jnp.concatenate([diag_re, diag_im], 1), jnp.concatenate([-diag_im, diag_re], 1)], 0
            )
            high, low = split_rows(both)
            lefts.append(jnp.concatenate([high, low], 0))
        for half in range(2):
            lanes = slice(half * 256, (half + 1) * 256)
            product = dot(turned, row_ref[partner, 0:144, lanes])
            real, imag = product[:256], product[256:]
            for qstep in range(2):
                screen_re, screen_im = tile_ref[qstep, 0, half], tile_ref[qstep, 1, half]
                mixed_re = (screen_re * real - screen_im * imag).astype(BF16)
                mixed_im = (screen_re * imag + screen_im * real).astype(BF16)
                total = dot(lefts[qstep], jnp.concatenate([mixed_re, mixed_im], 0))
                total = total[:16] + total[16:]
                far = row_ref[points[qstep], 144:176, lanes].astype(F32)
                far = far[:16] + far[16:]
                far_re, far_im = far[:8], far[8:]
                total_re, total_im = total[:8], total[8:]
                sum_re = far_re * total_re - far_im * total_im
                sum_im = far_re * total_im + far_im * total_re
                both = jnp.concatenate([sum_re, sum_im], 0)
                out_ref[points[qstep]] += both[:, :128] + both[:, 128:]
        return carry

    lax.fori_loop(0, KA, step, 0, unroll=4)


def call(kernel, outs, scratch, smem, *operands):
    smem_spec = [pl.BlockSpec(memory_space=pltpu.SMEM)] * smem
    vmem_spec = [pl.BlockSpec(memory_space=pltpu.VMEM)] * (len(operands) - smem)
    return pl.pallas_call(
        kernel,
        out_shape=[jax.ShapeDtypeStruct(shape, kind) for shape, kind in outs],
        in_specs=smem_spec + vmem_spec,
        out_specs=[pl.BlockSpec(memory_space=pltpu.VMEM)] * len(outs),
        scratch_shapes=scratch,
        compiler_params=pltpu.CompilerParams(vmem_limit_bytes=VMEM_BYTES),
    )(*operands)


def body(diag_waves, band_waves, screening, partner_map, grid_index):
    own = lax.axis_index("ga")
    exact_in, split_in, turned = [jnp.asarray(table) for table in make_tables()]
    place = (grid_index % N1) * N1 + grid_index // N1
    points = jnp.arange(KA, dtype=jnp.int32)
    owners = jnp.sum(
        jnp.where(partner_map[:, :, None] == points[None, None, :], points[None, :, None], 0), axis=1
    )
    band = band_waves[0].astype(BF16)
    band_rows = band.reshape(9, 2, GA, 4, 128).transpose(2, 1, 3, 0, 4).reshape(GA, 72, 128)
    band_rows = jnp.concatenate([band_rows, jnp.zeros((GA, 8, 128), BF16)], 1)
    band_columns = band.reshape(9, 2, KA, 2, 128).transpose(2, 1, 3, 0, 4).reshape(KA, 36, 128)
    diag = diag_waves[0].transpose(1, 0, 2)
    diag_high = lax.reduce_precision(diag, 8, 7)
    diag_low = (diag - diag_high).astype(BF16)
    diag_high = diag_high.astype(BF16)
    diag_both = jnp.stack([diag_high, diag_low])
    diag_columns = lax.dynamic_index_in_dim(diag_both, own, 2, keepdims=False)
    diag_columns = diag_columns.reshape(4, KA, 2, 128).transpose(1, 0, 2, 3).reshape(KA, 8, 128)
    columns = jnp.concatenate([band_columns, diag_columns, jnp.zeros((KA, 4, 128), BF16)], 1)
    diag_rows = lax.dynamic_slice_in_dim(diag_both.reshape(32, NG), own * 512, 512, 1)

    (packed,) = call(pack_kernel, [((GA, 592, 128), BF16)], [], 0, screening, band_rows)
    packed = lax.all_to_all(packed, "ga", 0, 0)
    work = [pltpu.VMEM((NG, 128), F32)] * 3
    spread, band_part = call(
        rows_kernel,
        [((KA * GA, 80, 128), BF16), ((144, 512), BF16)],
        work + [pltpu.VMEM((144, 512), F32)],
        1,
        place, packed, columns, exact_in, turned,
    )
    row_part = lax.all_gather(jnp.concatenate([band_part, diag_rows], 0), "ka", axis=0)
    spread = lax.all_to_all(spread, ALL, 0, 0)
    screen, column_part, diag_part = call(
        columns_kernel,
        [((NG, 128), BF16), ((KA, 144, 256), BF16), ((KA, 16, 256), F32)],
        work + [pltpu.VMEM((144, 256), F32)],
        1,
        place, spread, exact_in, split_in,
    )
    screen = lax.all_to_all(screen.reshape(KA, 256, 128), "ka", 0, 0)
    (partial,) = call(
        contract_kernel,
        [((KA, 16, 128), F32)],
        [pltpu.VMEM((2, 2, 2, 256, 256), F32)],
        1,
        owners, screen, row_part, column_part, diag_part,
    )
    value = jnp.sum(partial, axis=2)
    value = jnp.broadcast_to(value[:, None, :], (KA, GA, 16)).reshape(KA * GA, 16)
    value = jnp.sum(lax.all_to_all(value, ALL, 0, 0, tiled=True), axis=0)
    return value.reshape(2, 1, NBD) * (-1.0 / (QSTEPS * MB * math.sqrt(NG) * NG))


def solution(mesh):
    in_specs = (
        P("ka", None, None, None),
        P("ka", "ga", None, None),
        P(None, None, "ga", "ka"),
        P(),
        P(),
    )
    out_specs = P(None, "ka", None)
    return jax.shard_map(body, mesh=mesh, in_specs=in_specs, out_specs=out_specs, check_vma=False)
```

```python
import math

import jax
import jax.numpy as jnp
import numpy as np
from jax import lax
from jax.experimental import pallas as pl
from jax.experimental.pallas import tpu as pltpu
from jax.sharding import PartitionSpec as P

N1 = 64
NG = 4096
MB = 72
NBD = 8
QSTEPS = 2
KA = 16
GA = 8
F32 = jnp.float32
BF16 = jnp.bfloat16
VMEM_BYTES = 24 * 1024 * 1024
WHOLE_VMEM = 63 * 1024 * 1024
ALL = ("ka", "ga")


def split_table(table):
    high = table.astype(jnp.bfloat16)
    low = (table - high.astype(np.float64)).astype(jnp.bfloat16)
    return high, low


def make_tables():
    places = np.arange(N1)
    angle = (places[:, None] * places[None, :] % N1) * (2.0 * math.pi / N1)
    cos, sin = np.cos(angle), np.sin(angle)
    high, low = split_table(np.concatenate([cos, sin], 0))
    exact_in = np.concatenate([high, low], 1)
    split_in = np.concatenate([high, high, low], 1)
    wide = np.concatenate([cos, sin], 1)
    block = np.zeros((2 * N1, 4 * N1))
    block[:N1, : 2 * N1] = wide
    block[N1:, 2 * N1 :] = wide
    high, low = split_table(block)
    turned = np.concatenate([high, high, low], 0)
    return exact_in, split_in, turned


def lane_sign(rows, first):
    lane = lax.broadcasted_iota(jnp.int32, (rows, 128), 1)
    return jnp.where(lane < 64, first, -first).astype(F32)


def swap_halves(x):
    return pltpu.roll(x, 64, 1)


def split_rows(x):
    high = x.astype(BF16)
    low = (x - high.astype(F32)).astype(BF16)
    return high, low


def dot(a, b):
    return jnp.dot(a, b, preferred_element_type=F32)


def pack_kernel(own_ref, w_hbm, band_hbm, diag_hbm, out_ref, columns_ref, rows_ref, w_ref, band_ref, diag_ref, sems):
    own = own_ref[0]
    band_copy = pltpu.make_async_copy(band_hbm, band_ref, sems.at[0])
    diag_copy = pltpu.make_async_copy(diag_hbm.at[own], diag_ref, sems.at[1])
    band_copy.start()
    diag_copy.start()
    w_copies = []
    for block in range(4):
        lines = pl.ds(block * 128, 128)
        copy = pltpu.make_async_copy(w_hbm.at[:, :, lines], w_ref.at[:, :, lines], sems.at[2 + block])
        copy.start()
        w_copies.append(copy)
    band_copy.wait()
    diag_copy.wait()
    rows_ref[16:24, :] = jnp.zeros((8, NG), F32)
    for band in range(8):
        rows_ref[band : band + 1, :] = band_ref[band, 0:1, :]
        rows_ref[8 + band : 9 + band, :] = band_ref[band, 1:2, :]
    rows_ref[16:18, :] = band_ref[8]
    diag = diag_ref[...]
    high = diag.astype(BF16).astype(F32)
    rows_ref[18:20, :] = high
    rows_ref[20:22, :] = diag - high
    for pair in range(16):
        lanes = [slice((pair * 2 + side) * 128, (pair * 2 + side + 1) * 128) for side in range(2)]
        block = jnp.concatenate([rows_ref[:, lane] for lane in lanes], 0).astype(BF16)
        columns_ref[2 * pair] = block
        columns_ref[2 * pair + 1] = block
        first = 512 + pair % 2 * 48
        out_ref[pair // 2, first : first + 48, :] = block
    lane = lax.broadcasted_iota(jnp.int32, (128, 128), 1) // 32
    for block in range(4):
        w_copies[block].wait()
        lines = slice(block * 128, (block + 1) * 128)
        for dest in range(GA):
            half, place = dest // 4, dest % 4
            total = None
            for slot in range(4):
                part, qstep = slot // 2, slot % 2
                source = w_ref[qstep, part, lines, half * 128 : (half + 1) * 128]
                shift = (slot - place) * 32 % 128
                moved = pltpu.roll(source, shift, 1) if shift else source
                total = moved if total is None else jnp.where(lane == slot, moved, total)
            out_ref[dest, lines, :] = total.astype(BF16)


def scatter_rows(place_ref, from_ref, to_ref):
    def step(block, carry):
        for inner in range(64):
            row = block * 64 + inner
            to_ref[pl.ds(place_ref[row], 1), :] = from_ref[pl.ds(row, 1), :]
        return carry

    lax.fori_loop(0, NG // 64, step, 0)


def first_axis(exact_ref, grid_ref, half_ref, sign):
    table = exact_ref[...]
    signs = lane_sign(64, sign)

    def step(pair, carry):
        rows = grid_ref[pl.ds(pl.multiple_of(pair * 128, 128), 128), :].astype(BF16)
        left, right = rows[:64], rows[64:]
        stacked = jnp.concatenate(
            [jnp.concatenate([left, left], 0), jnp.concatenate([right, right], 0)], 1
        )
        out = dot(table, stacked)
        for side in range(2):
            piece = out[:, side * 128 : (side + 1) * 128]
            mixed = piece[:64] + signs * swap_halves(piece[64:])
            half_ref[pl.ds(pl.multiple_of(pair * 128 + side * 64, 64), 64), :] = mixed
        return carry

    lax.fori_loop(0, 32, step, 0, unroll=16)


def rows_kernel(place_ref, got_ref, exact_ref, turned_ref, out_ref, flat_ref, grid_ref, half_ref):
    for source in range(GA):
        flat_ref[source * 512 : (source + 1) * 512, :] = got_ref[source, 0:512, :].astype(F32)
    scatter_rows(place_ref, flat_ref, grid_ref)
    first_axis(exact_ref, grid_ref, half_ref, -1.0)
    signs = lane_sign(64, -1.0)
    table = turned_ref[...]

    def step(pair, carry):
        both = jnp.concatenate(
            [half_ref[pl.ds(pair * 2 + side, 64, stride=64), :] for side in range(2)], 0
        )
        high, low = split_rows(both.T)
        out = dot(jnp.concatenate([high, low, high], 1), table)
        for side in range(2):
            piece = out[:, side * 128 : (side + 1) * 128]
            mixed = (piece[:64] + signs * swap_halves(piece[64:])).astype(BF16)
            first = pair * 2 + side
            for qstep in range(2):
                dest = (qstep * 8 + first % 8) * GA + first // 8
                out_ref[dest, 0:32, :] = mixed[qstep * 32 : (qstep + 1) * 32]
        return carry

    lax.fori_loop(0, 32, step, 0, unroll=16)


def columns_kernel(place_ref, got_ref, exact_ref, split_ref, out_ref, flat_ref, grid_ref, half_ref):
    def unpack(index, carry):
        flat_ref[pl.ds(pl.multiple_of(index * 32, 32), 32), :] = got_ref[index, 0:32, :].astype(F32)
        return carry

    lax.fori_loop(0, KA * GA, unpack, 0, unroll=16)
    scatter_rows(place_ref, flat_ref, grid_ref)
    first_axis(exact_ref, grid_ref, half_ref, 1.0)
    signs = lane_sign(64, 1.0)
    table = split_ref[...]

    def step(pair, carry):
        columns = []
        for side in range(2):
            high, low = split_rows(half_ref[pl.ds(pair * 2 + side, 64, stride=64), :])
            columns.append(jnp.concatenate([high, low, high], 0))
        out = dot(table, jnp.concatenate(columns, 1))
        for side in range(2):
            piece = out[:, side * 128 : (side + 1) * 128]
            mixed = piece[:64] + signs * swap_halves(piece[64:])
            out_ref[pl.ds(pl.multiple_of(pair * 128 + side * 64, 64), 64), :] = mixed.astype(BF16)
        return carry

    lax.fori_loop(0, 32, step, 0, unroll=16)


def pick_diag(rows):
    line = lax.broadcasted_iota(jnp.int32, (16, 192), 0)
    place = lax.broadcasted_iota(jnp.int32, (16, 192), 1)
    first = line % 8 * 24 + 18 + line // 8
    pick = jnp.where((place == first) | (place == first + 2), 1.0, 0.0).astype(BF16)
    return dot(pick, rows)


def row_side_kernel(own_ref, *refs):
    *part_refs, rows_ref, diag_ref = refs
    own = own_ref[0]
    z_own, x_own, c_own = own // 8, own // 2 % 4, own % 2
    for flip in range(2):
        for shift in range(4):
            from_ref = part_refs[flip * 4 + shift]
            for turn in range(2):
                point = (z_own + turn) % 2 * 8 + (x_own + 4 - shift) % 4 * 2 + (c_own + flip) % 2
                for pair in range(4):
                    blocks = []
                    for source in (2 * pair, 2 * pair + 1):
                        block = from_ref[turn, source].astype(F32)
                        blocks.append(
                            jnp.concatenate([block[24 * group : 24 * group + 24] for group in range(4)], 1)
                        )
                    rows_ref[point, 48 * pair : 48 * pair + 48, :] = jnp.concatenate(blocks, 0).astype(BF16)

    def step(point, carry):
        diag_ref[point] = pick_diag(rows_ref[point])
        return carry

    lax.fori_loop(0, KA, step, 0, unroll=4)


def column_side_kernel(own_ref, *refs):
    *part_refs, turned_ref, left_ref, whole_ref = refs
    y_own = own_ref[0] // 2
    for shift in range(4):
        whole_ref[(y_own + 4 - shift) % 4] = part_refs[shift][...]
    line = lax.broadcasted_iota(jnp.int32, (8, 256), 0)

    def step(point, carry):
        plain, straight, crossed = [], [], []
        for source in range(GA):
            block = whole_ref[source // 2, 2 * point + source % 2].astype(F32)
            block = jnp.concatenate([block[:24], block[24:]], 1)
            plain.append(block)
            real, imag, rest = block[:8], block[8:16], block[16:]
            straight += [real, imag, jnp.where(line < 2, rest, 0.0)]
            swapped = jnp.where(line == 0, pltpu.roll(rest, 7, 0), -pltpu.roll(rest, 1, 0))
            crossed += [imag, -real, jnp.where(line < 2, swapped, 0.0)]
        diag = pick_diag(jnp.concatenate(plain, 0).astype(BF16))
        diag_re, diag_im = diag[:8], diag[8:]
        both = jnp.concatenate(
            [jnp.concatenate([diag_re, diag_im], 1), jnp.concatenate([-diag_im, diag_re], 1)], 0
        )
        high, low = split_rows(both)
        left_ref[point] = jnp.concatenate([high, low], 0)
        turned_ref[point, 0:256, :] = jnp.concatenate(straight, 0).T.astype(BF16)
        turned_ref[point, 256:512, :] = jnp.concatenate(crossed, 0).T.astype(BF16)
        return carry

    lax.fori_loop(0, KA, step, 0, unroll=2)


def fill_tiles(screen_ref, tile_ref):
    lane = lax.broadcasted_iota(jnp.int32, (256, 128), 1) < 64
    for qstep in range(2):
        for group in range(4):
            even = screen_ref[qstep * 8 + group * 2].astype(F32)
            odd = screen_ref[qstep * 8 + group * 2 + 1].astype(F32)
            lanes = slice(group % 2 * 128, (group % 2 + 1) * 128)
            tile_ref[qstep, 0, group // 2, :, lanes] = jnp.where(lane, even, swap_halves(odd))
            tile_ref[qstep, 1, group // 2, :, lanes] = jnp.where(lane, swap_halves(even), odd)


def contract_kernel(point_ref, screen_ref, row_ref, far_ref, turned_ref, left_ref, out_ref, sum_ref, tile_ref):
    first = pl.program_id(0) * 4

    @pl.when(first == 0)
    def _():
        sum_ref[...] = jnp.zeros_like(sum_ref)
        fill_tiles(screen_ref, tile_ref)

    for inner in range(4):
        turned = turned_ref[inner]
        for half in range(2):
            lanes = slice(half * 256, (half + 1) * 256)
            product = dot(turned, row_ref[inner, :, lanes])
            real, imag = product[:256], product[256:]
            for qstep in range(2):
                point = point_ref[qstep, first + inner]
                screen_re, screen_im = tile_ref[qstep, 0, half], tile_ref[qstep, 1, half]
                mixed_re = (screen_re * real - screen_im * imag).astype(BF16)
                mixed_im = (screen_re * imag + screen_im * real).astype(BF16)
                total = dot(left_ref[point], jnp.concatenate([mixed_re, mixed_im], 0))
                total = total[:16] + total[16:]
                far = far_ref[point, :, lanes]
                far_re, far_im = far[:8], far[8:]
                total_re, total_im = total[:8], total[8:]
                sum_re = far_re * total_re - far_im * total_im
                sum_im = far_re * total_im + far_im * total_re
                both = jnp.concatenate([sum_re, sum_im], 0)
                sum_ref[point] += both[:, :128] + both[:, 128:]

    @pl.when(first == KA - 4)
    def _():
        value = jnp.sum(sum_ref[...], axis=2)
        out_ref[...] = jnp.broadcast_to(value[:, None, :], (KA, GA, 16))


def call(kernel, outs, scratch, smem, *operands, space=pltpu.VMEM, limit=VMEM_BYTES):
    smem_spec = [pl.BlockSpec(memory_space=pltpu.SMEM)] * smem
    vmem_spec = [pl.BlockSpec(memory_space=space)] * (len(operands) - smem)
    return pl.pallas_call(
        kernel,
        out_shape=[jax.ShapeDtypeStruct(shape, kind) for shape, kind in outs],
        in_specs=smem_spec + vmem_spec,
        out_specs=[pl.BlockSpec(memory_space=pltpu.VMEM)] * len(outs),
        scratch_shapes=scratch,
        compiler_params=pltpu.CompilerParams(vmem_limit_bytes=limit),
    )(*operands)


def flip_z(part):
    return lax.ppermute(part, "ka", [(index, index ^ 8) for index in range(KA)])


def along_x(part):
    parts = []
    for shift in range(1, 4):
        along = [(index, index // 8 * 8 + (index + 2 * shift) % 8) for index in range(KA)]
        parts.append(lax.ppermute(part, "ka", along))
    return parts


def along_y(part):
    parts = [part]
    for shift in range(1, 4):
        along = [(index, (index + 2 * shift) % GA) for index in range(GA)]
        parts.append(lax.ppermute(part, "ga", along))
    return parts


def flip_core(part):
    return lax.ppermute(part, "ka", [(index, index ^ 1) for index in range(KA)])


def body(diag_waves, band_waves, screening, partner_map, grid_index):
    own_k = lax.axis_index("ka").astype(jnp.int32).reshape(1)
    own_g = lax.axis_index("ga").astype(jnp.int32).reshape(1)
    exact_in, split_in, turned = [jnp.asarray(table) for table in make_tables()]
    place = (grid_index % N1) * N1 + grid_index // N1
    points = jnp.arange(KA, dtype=jnp.int32)
    owners = jnp.sum(
        jnp.where(partner_map[:, :, None] == points[None, None, :], points[None, :, None], 0), axis=1
    )
    work = [pltpu.VMEM((NG, 128), F32)] * 3
    packed, columns = call(
        pack_kernel,
        [((GA, 608, 128), BF16), ((2 * KA, 48, 128), BF16)],
        [
            pltpu.VMEM((24, NG), F32),
            pltpu.VMEM((2, 2, 512, 256), F32),
            pltpu.VMEM((9, 2, NG), F32),
            pltpu.VMEM((2, NG), F32),
            pltpu.SemaphoreType.DMA((6,)),
        ],
        1,
        own_g, screening, band_waves[0], diag_waves[0],
        space=pltpu.HBM,
        limit=WHOLE_VMEM,
    )
    packed = lax.all_to_all(packed, "ga", 0, 0)
    packed, columns = lax.optimization_barrier((packed, columns))
    planes = [[ka * GA + 2 * y + z for ka in range(KA) for z in range(2)] for y in range(4)]
    columns = lax.all_to_all(columns, ALL, 0, 0, axis_index_groups=planes)
    own_part = packed[:, 512:608]
    flipped_part = flip_z(own_part)
    (spread,) = call(
        rows_kernel, [((KA * GA, 32, 128), BF16)], work, 1, place, packed, exact_in, turned
    )
    spread, flipped_part, columns = lax.optimization_barrier((spread, flipped_part, columns))
    own_part = jnp.stack([own_part, flipped_part])
    parts = along_x(own_part)
    column_parts = along_y(columns)
    spread = lax.all_to_all(spread, ALL, 0, 0)
    (screen,) = call(
        columns_kernel, [((NG, 128), BF16)], work, 1, place, spread, exact_in, split_in
    )
    parts, column_parts, screen = lax.optimization_barrier((parts, column_parts, screen))
    screen = lax.all_to_all(screen.reshape(KA, 256, 128), "ka", 0, 0)
    parts = [own_part, *parts]
    parts += [flip_core(part) for part in parts]
    rows, far = call(
        row_side_kernel, [((KA, 192, 512), BF16), ((KA, 16, 512), F32)], [], 1, own_k, *parts
    )
    near, left = call(
        column_side_kernel, [((KA, 512, 192), BF16), ((KA, 32, 512), BF16)],
        [pltpu.VMEM((4, 2 * KA, 48, 128), BF16)],
        1,
        own_g, *column_parts,
    )
    partial = pl.pallas_call(
        contract_kernel,
        out_shape=jax.ShapeDtypeStruct((KA, GA, 16), F32),
        grid=(4,),
        in_specs=[
            pl.BlockSpec(memory_space=pltpu.SMEM),
            pl.BlockSpec((KA, 256, 128), lambda step: (0, 0, 0)),
            pl.BlockSpec((4, 192, 512), lambda step: (step, 0, 0)),
            pl.BlockSpec((KA, 16, 512), lambda step: (0, 0, 0)),
            pl.BlockSpec((4, 512, 192), lambda step: (step, 0, 0)),
            pl.BlockSpec((KA, 32, 512), lambda step: (0, 0, 0)),
        ],
        out_specs=pl.BlockSpec((KA, GA, 16), lambda step: (0, 0, 0)),
        scratch_shapes=[pltpu.VMEM((KA, 16, 128), F32), pltpu.VMEM((2, 2, 2, 256, 256), F32)],
        compiler_params=pltpu.CompilerParams(vmem_limit_bytes=WHOLE_VMEM),
    )(owners, screen, rows, far, near, left)
    value = partial.reshape(KA * GA, 16)
    value = jnp.sum(lax.all_to_all(value, ALL, 0, 0, tiled=True), axis=0)
    return value.reshape(2, 1, NBD) * (-1.0 / (QSTEPS * MB * math.sqrt(NG) * NG))


def solution(mesh):
    in_specs = (
        P("ka", None, None, None),
        P("ka", "ga", None, None),
        P(None, None, "ga", "ka"),
        P(),
        P(),
    )
    out_specs = P(None, "ka", None)
    return jax.shard_map(body, mesh=mesh, in_specs=in_specs, out_specs=out_specs, check_vma=False)
```

```python
import math

import jax
import jax.numpy as jnp
import numpy as np
from jax import lax
from jax.experimental import pallas as pl
from jax.experimental.pallas import tpu as pltpu
from jax.sharding import PartitionSpec as P

N1 = 64
NG = 4096
MB = 72
NBD = 8
QSTEPS = 2
KA = 16
GA = 8
F32 = jnp.float32
BF16 = jnp.bfloat16
VMEM_BYTES = 24 * 1024 * 1024
WHOLE_VMEM = 63 * 1024 * 1024
ALL = ("ka", "ga")


def split_table(table):
    high = table.astype(jnp.bfloat16)
    low = (table - high.astype(np.float64)).astype(jnp.bfloat16)
    return high, low


def make_tables():
    places = np.arange(N1)
    angle = (places[:, None] * places[None, :] % N1) * (2.0 * math.pi / N1)
    cos, sin = np.cos(angle), np.sin(angle)
    high, low = split_table(np.concatenate([cos, sin], 0))
    exact_in = np.concatenate([high, low], 1)
    split_in = np.concatenate([high, high, low], 1)
    wide = np.concatenate([cos, sin], 1)
    block = np.zeros((2 * N1, 4 * N1))
    block[:N1, : 2 * N1] = wide
    block[N1:, 2 * N1 :] = wide
    high, low = split_table(block)
    turned = np.concatenate([high, high, low], 0)
    return exact_in, split_in, turned


def lane_sign(rows, first):
    lane = lax.broadcasted_iota(jnp.int32, (rows, 128), 1)
    return jnp.where(lane < 64, first, -first).astype(F32)


def swap_halves(x):
    return pltpu.roll(x, 64, 1)


def split_rows(x):
    high = x.astype(BF16)
    low = (x - high.astype(F32)).astype(BF16)
    return high, low


def dot(a, b):
    return jnp.dot(a, b, preferred_element_type=F32)


def pack_kernel(own_ref, w_hbm, band_hbm, diag_hbm, out_ref, columns_ref, rows_ref, w_ref, band_ref, diag_ref, sems):
    own = own_ref[0]
    band_copy = pltpu.make_async_copy(band_hbm, band_ref, sems.at[0])
    diag_copy = pltpu.make_async_copy(diag_hbm.at[own], diag_ref, sems.at[1])
    band_copy.start()
    diag_copy.start()
    w_copies = []
    for block in range(4):
        lines = pl.ds(block * 128, 128)
        copy = pltpu.make_async_copy(w_hbm.at[:, :, lines], w_ref.at[:, :, lines], sems.at[2 + block])
        copy.start()
        w_copies.append(copy)
    band_copy.wait()
    diag_copy.wait()
    rows_ref[16:24, :] = jnp.zeros((8, NG), F32)
    for band in range(8):
        rows_ref[band : band + 1, :] = band_ref[band, 0:1, :]
        rows_ref[8 + band : 9 + band, :] = band_ref[band, 1:2, :]
    rows_ref[16:18, :] = band_ref[8]
    diag = diag_ref[...]
    high = diag.astype(BF16).astype(F32)
    rows_ref[18:20, :] = high
    rows_ref[20:22, :] = diag - high
    for pair in range(16):
        lanes = [slice((pair * 2 + side) * 128, (pair * 2 + side + 1) * 128) for side in range(2)]
        block = jnp.concatenate([rows_ref[:, lane] for lane in lanes], 0).astype(BF16)
        columns_ref[2 * pair] = block
        columns_ref[2 * pair + 1] = block
        first = 512 + pair % 2 * 48
        out_ref[pair // 2, first : first + 48, :] = block
    lane = lax.broadcasted_iota(jnp.int32, (128, 128), 1) // 32
    for block in range(4):
        w_copies[block].wait()
        lines = slice(block * 128, (block + 1) * 128)
        for dest in range(GA):
            half, place = dest // 4, dest % 4
            total = None
            for slot in range(4):
                part, qstep = slot // 2, slot % 2
                source = w_ref[qstep, part, lines, half * 128 : (half + 1) * 128]
                shift = (slot - place) * 32 % 128
                moved = pltpu.roll(source, shift, 1) if shift else source
                total = moved if total is None else jnp.where(lane == slot, moved, total)
            out_ref[dest, lines, :] = total.astype(BF16)


def scatter_rows(place_ref, from_ref, to_ref):
    def step(block, carry):
        for inner in range(256):
            row = block * 256 + inner
            to_ref[pl.ds(place_ref[row], 1), :] = from_ref[pl.ds(row, 1), :]
        return carry

    lax.fori_loop(0, NG // 256, step, 0)


def first_axis(exact_ref, grid_ref, half_ref, sign):
    table = exact_ref[...]
    signs = lane_sign(64, sign)

    def step(pair, carry):
        rows = grid_ref[pl.ds(pl.multiple_of(pair * 128, 128), 128), :].astype(BF16)
        left, right = rows[:64], rows[64:]
        stacked = jnp.concatenate(
            [jnp.concatenate([left, left], 0), jnp.concatenate([right, right], 0)], 1
        )
        out = dot(table, stacked)
        for side in range(2):
            piece = out[:, side * 128 : (side + 1) * 128]
            mixed = piece[:64] + signs * swap_halves(piece[64:])
            half_ref[pl.ds(pl.multiple_of(pair * 128 + side * 64, 64), 64), :] = mixed
        return carry

    lax.fori_loop(0, 32, step, 0, unroll=32)


def rows_kernel(place_ref, got_ref, exact_ref, turned_ref, out_hbm, out_ref, flat_ref, grid_ref, half_ref, sems):
    for source in range(GA):
        flat_ref[source * 512 : (source + 1) * 512, :] = got_ref[source, 0:512, :].astype(F32)
    scatter_rows(place_ref, flat_ref, grid_ref)
    first_axis(exact_ref, grid_ref, half_ref, -1.0)
    signs = lane_sign(64, -1.0)
    table = turned_ref[...]
    sent = []
    for owner in range(GA):
        for duo in range(2):
            first = owner * 8 + duo * 4
            lefts = []
            for pair in range(2):
                both = jnp.concatenate(
                    [half_ref[pl.ds(first + pair * 2 + side, 64, stride=64), :] for side in range(2)], 0
                )
                high, low = split_rows(both.T)
                lefts.append(jnp.concatenate([high, low, high], 1))
            out = dot(jnp.concatenate(lefts, 0), table)
            for place in range(4):
                pair, side = place // 2, place % 2
                piece = out[pair * 128 : (pair + 1) * 128, side * 128 : (side + 1) * 128]
                mixed = (piece[:64] + signs * swap_halves(piece[64:])).astype(BF16)
                for qstep in range(2):
                    out_ref[owner, qstep * 8 + duo * 4 + place] = mixed[qstep * 32 : (qstep + 1) * 32]
        copy = pltpu.make_async_copy(out_ref.at[owner], out_hbm.at[:, owner], sems.at[owner])
        copy.start()
        sent.append(copy)
    for copy in sent:
        copy.wait()


def columns_kernel(place_ref, got_ref, exact_ref, split_ref, out_hbm, out_ref, flat_ref, grid_ref, half_ref, sems):
    def unpack(index, carry):
        flat_ref[pl.ds(pl.multiple_of(index * 32, 32), 32), :] = got_ref[index, 0:32, :].astype(F32)
        return carry

    lax.fori_loop(0, KA * GA, unpack, 0, unroll=16)
    scatter_rows(place_ref, flat_ref, grid_ref)
    first_axis(exact_ref, grid_ref, half_ref, 1.0)
    signs = lane_sign(64, 1.0)
    table = split_ref[...]

    sent = []
    for pair in range(32):
        columns = []
        for side in range(2):
            high, low = split_rows(half_ref[pl.ds(pair * 2 + side, 64, stride=64), :])
            columns.append(jnp.concatenate([high, low, high], 0))
        out = dot(table, jnp.concatenate(columns, 1))
        for side in range(2):
            piece = out[:, side * 128 : (side + 1) * 128]
            mixed = piece[:64] + signs * swap_halves(piece[64:])
            out_ref[pair * 128 + side * 64 : pair * 128 + side * 64 + 64, :] = mixed.astype(BF16)
        if pair % 8 == 7:
            lines = pl.ds((pair - 7) * 128, 1024)
            copy = pltpu.make_async_copy(out_ref.at[lines], out_hbm.at[lines], sems.at[pair // 8])
            copy.start()
            sent.append(copy)
    for copy in sent:
        copy.wait()


def pick_diag(rows):
    line = lax.broadcasted_iota(jnp.int32, (16, 192), 0)
    place = lax.broadcasted_iota(jnp.int32, (16, 192), 1)
    first = line % 8 * 24 + 18 + line // 8
    pick = jnp.where((place == first) | (place == first + 2), 1.0, 0.0).astype(BF16)
    return dot(pick, rows)


def row_side_kernel(own_ref, *refs):
    *part_refs, rows_ref, diag_ref = refs
    own = own_ref[0]
    z_own, x_own, c_own = own // 8, own // 2 % 4, own % 2
    for flip in range(2):
        for shift in range(4):
            for turn in range(2):
                own_pair, up, down, *far = part_refs[flip * 5 : flip * 5 + 5]
                from_ref = (own_pair, up, far[turn], down)[shift]
                point = (z_own + turn) % 2 * 8 + (x_own + 4 - shift) % 4 * 2 + (c_own + flip) % 2
                for pair in range(4):
                    blocks = []
                    for source in (2 * pair, 2 * pair + 1):
                        block = (from_ref[source] if shift == 2 else from_ref[turn, source]).astype(F32)
                        blocks.append(
                            jnp.concatenate([block[24 * group : 24 * group + 24] for group in range(4)], 1)
                        )
                    rows_ref[point, 48 * pair : 48 * pair + 48, :] = jnp.concatenate(blocks, 0).astype(BF16)

    def step(point, carry):
        diag_ref[point] = pick_diag(rows_ref[point])
        return carry

    lax.fori_loop(0, KA, step, 0, unroll=4)


def column_side_kernel(own_ref, *refs):
    *part_refs, turned_ref, left_ref, whole_ref = refs
    y_own = own_ref[0] // 2
    for shift in range(4):
        whole_ref[(y_own + 4 - shift) % 4] = part_refs[shift][...]
    line = lax.broadcasted_iota(jnp.int32, (8, 256), 0)

    def step(point, carry):
        plain, straight, crossed = [], [], []
        for source in range(GA):
            block = whole_ref[source // 2, 2 * point + source % 2].astype(F32)
            block = jnp.concatenate([block[:24], block[24:]], 1)
            plain.append(block)
            real, imag, rest = block[:8], block[8:16], block[16:]
            straight += [real, imag, jnp.where(line < 2, rest, 0.0)]
            swapped = jnp.where(line == 0, pltpu.roll(rest, 7, 0), -pltpu.roll(rest, 1, 0))
            crossed += [imag, -real, jnp.where(line < 2, swapped, 0.0)]
        diag = pick_diag(jnp.concatenate(plain, 0).astype(BF16))
        diag_re, diag_im = diag[:8], diag[8:]
        both = jnp.concatenate(
            [jnp.concatenate([diag_re, diag_im], 1), jnp.concatenate([-diag_im, diag_re], 1)], 0
        )
        high, low = split_rows(both)
        left_ref[point] = jnp.concatenate([high, low], 0)
        turned_ref[point, 0:256, :] = jnp.concatenate(straight, 0).T.astype(BF16)
        turned_ref[point, 256:512, :] = jnp.concatenate(crossed, 0).T.astype(BF16)
        return carry

    lax.fori_loop(0, KA, step, 0, unroll=2)


def fill_tiles(screen_ref, tile_ref):
    lane = lax.broadcasted_iota(jnp.int32, (256, 128), 1) < 64
    for qstep in range(2):
        for group in range(4):
            even = screen_ref[qstep * 8 + group * 2].astype(F32)
            odd = screen_ref[qstep * 8 + group * 2 + 1].astype(F32)
            lanes = slice(group % 2 * 128, (group % 2 + 1) * 128)
            tile_ref[qstep, 0, group // 2, :, lanes] = jnp.where(lane, even, swap_halves(odd))
            tile_ref[qstep, 1, group // 2, :, lanes] = jnp.where(lane, swap_halves(even), odd)


def contract_kernel(point_ref, screen_ref, row_ref, far_ref, turned_ref, left_ref, out_ref, sum_ref, tile_ref):
    first = pl.program_id(0) * 4

    @pl.when(first == 0)
    def _():
        sum_ref[...] = jnp.zeros_like(sum_ref)
        fill_tiles(screen_ref, tile_ref)

    for inner in range(4):
        turned = turned_ref[inner]
        for half in range(2):
            lanes = slice(half * 256, (half + 1) * 256)
            product = dot(turned, row_ref[inner, :, lanes])
            real, imag = product[:256], product[256:]
            for qstep in range(2):
                point = point_ref[qstep, first + inner]
                screen_re, screen_im = tile_ref[qstep, 0, half], tile_ref[qstep, 1, half]
                mixed_re = (screen_re * real - screen_im * imag).astype(BF16)
                mixed_im = (screen_re * imag + screen_im * real).astype(BF16)
                total = dot(left_ref[point], jnp.concatenate([mixed_re, mixed_im], 0))
                total = total[:16] + total[16:]
                far = far_ref[point, :, lanes]
                far_re, far_im = far[:8], far[8:]
                total_re, total_im = total[:8], total[8:]
                sum_re = far_re * total_re - far_im * total_im
                sum_im = far_re * total_im + far_im * total_re
                both = jnp.concatenate([sum_re, sum_im], 0)
                sum_ref[point] += both[:, :128] + both[:, 128:]

    @pl.when(first == KA - 4)
    def _():
        value = jnp.sum(sum_ref[...], axis=2)
        out_ref[...] = jnp.broadcast_to(value[:, None, :], (KA, GA, 16))


def call(kernel, outs, scratch, smem, *operands, space=pltpu.VMEM, limit=VMEM_BYTES, far_outs=0):
    smem_spec = [pl.BlockSpec(memory_space=pltpu.SMEM)] * smem
    vmem_spec = [pl.BlockSpec(memory_space=space)] * (len(operands) - smem)
    return pl.pallas_call(
        kernel,
        out_shape=[jax.ShapeDtypeStruct(shape, kind) for shape, kind in outs],
        in_specs=smem_spec + vmem_spec,
        out_specs=[
            pl.BlockSpec(memory_space=pl.ANY if index < far_outs else pltpu.VMEM) for index in range(len(outs))
        ],
        scratch_shapes=scratch,
        compiler_params=pltpu.CompilerParams(vmem_limit_bytes=limit),
    )(*operands)


def flip_z(part):
    return lax.ppermute(part, "ka", [(index, index ^ 8) for index in range(KA)])


def along_x(part, shift):
    return lax.ppermute(part, "ka", [(index, index // 8 * 8 + (index + 2 * shift) % 8) for index in range(KA)])


def along_y(part):
    parts = [part]
    for shift in range(1, 4):
        along = [(index, (index + 2 * shift) % GA) for index in range(GA)]
        parts.append(lax.ppermute(part, "ga", along))
    return parts


def flip_core(part):
    return lax.ppermute(part, "ka", [(index, index ^ 1) for index in range(KA)])


def body(diag_waves, band_waves, screening, partner_map, grid_index):
    own_k = lax.axis_index("ka").astype(jnp.int32).reshape(1)
    own_g = lax.axis_index("ga").astype(jnp.int32).reshape(1)
    exact_in, split_in, turned = [jnp.asarray(table) for table in make_tables()]
    place = (grid_index % N1) * N1 + grid_index // N1
    points = jnp.arange(KA, dtype=jnp.int32)
    owners = jnp.sum(
        jnp.where(partner_map[:, :, None] == points[None, None, :], points[None, :, None], 0), axis=1
    )
    work = [pltpu.VMEM((NG, 128), F32)] * 3
    packed, columns = call(
        pack_kernel,
        [((GA, 608, 128), BF16), ((2 * KA, 48, 128), BF16)],
        [
            pltpu.VMEM((24, NG), F32),
            pltpu.VMEM((2, 2, 512, 256), F32),
            pltpu.VMEM((9, 2, NG), F32),
            pltpu.VMEM((2, NG), F32),
            pltpu.SemaphoreType.DMA((6,)),
        ],
        1,
        own_g, screening, band_waves[0], diag_waves[0],
        space=pltpu.HBM,
        limit=WHOLE_VMEM,
    )
    packed = lax.all_to_all(packed, "ga", 0, 0)
    packed, columns = lax.optimization_barrier((packed, columns))
    planes = [[ka * GA + 2 * y + z for ka in range(KA) for z in range(2)] for y in range(4)]
    columns = lax.all_to_all(columns, ALL, 0, 0, axis_index_groups=planes)
    own_part = packed[:, 512:608]
    flipped_part = flip_z(own_part)
    far_part = along_x(own_part, 2)
    (spread,) = call(
        rows_kernel,
        [((KA, GA, 32, 128), BF16)],
        [pltpu.VMEM((GA, KA, 32, 128), BF16), *work, pltpu.SemaphoreType.DMA((GA,))],
        1,
        place, packed, exact_in, turned,
        far_outs=1,
    )
    spread = spread.reshape(KA * GA, 32, 128)
    spread, flipped_part, far_part, columns = lax.optimization_barrier((spread, flipped_part, far_part, columns))
    own_part = jnp.stack([own_part, flipped_part])
    parts = [along_x(own_part, 1), along_x(own_part, 3)]
    column_parts = along_y(columns)
    spread = lax.all_to_all(spread, ALL, 0, 0)
    spread, far_part = lax.optimization_barrier((spread, far_part))
    far_parts = [far_part, flip_z(far_part)]
    (screen,) = call(
        columns_kernel,
        [((NG, 128), BF16)],
        [pltpu.VMEM((NG, 128), BF16), *work, pltpu.SemaphoreType.DMA((4,))],
        1,
        place, spread, exact_in, split_in,
        far_outs=1,
    )
    parts, column_parts, far_parts, screen = lax.optimization_barrier((parts, column_parts, far_parts, screen))
    screen = lax.all_to_all(screen.reshape(KA, 256, 128), "ka", 0, 0)
    parts = [own_part, *parts, *far_parts]
    parts += [flip_core(part) for part in parts]
    rows, far = call(
        row_side_kernel, [((KA, 192, 512), BF16), ((KA, 16, 512), F32)], [], 1, own_k, *parts
    )
    near, left = call(
        column_side_kernel, [((KA, 512, 192), BF16), ((KA, 32, 512), BF16)],
        [pltpu.VMEM((4, 2 * KA, 48, 128), BF16)],
        1,
        own_g, *column_parts,
    )
    partial = pl.pallas_call(
        contract_kernel,
        out_shape=jax.ShapeDtypeStruct((KA, GA, 16), F32),
        grid=(4,),
        in_specs=[
            pl.BlockSpec(memory_space=pltpu.SMEM),
            pl.BlockSpec((KA, 256, 128), lambda step: (0, 0, 0)),
            pl.BlockSpec((4, 192, 512), lambda step: (step, 0, 0)),
            pl.BlockSpec((KA, 16, 512), lambda step: (0, 0, 0)),
            pl.BlockSpec((4, 512, 192), lambda step: (step, 0, 0)),
            pl.BlockSpec((KA, 32, 512), lambda step: (0, 0, 0)),
        ],
        out_specs=pl.BlockSpec((KA, GA, 16), lambda step: (0, 0, 0)),
        scratch_shapes=[pltpu.VMEM((KA, 16, 128), F32), pltpu.VMEM((2, 2, 2, 256, 256), F32)],
        compiler_params=pltpu.CompilerParams(vmem_limit_bytes=WHOLE_VMEM),
    )(owners, screen, rows, far, near, left)
    value = partial.reshape(KA * GA, 16)
    value = jnp.sum(lax.all_to_all(value, ALL, 0, 0, tiled=True), axis=0)
    return value.reshape(2, 1, NBD) * (-1.0 / (QSTEPS * MB * math.sqrt(NG) * NG))


def solution(mesh):
    in_specs = (
        P("ka", None, None, None),
        P("ka", "ga", None, None),
        P(None, None, "ga", "ka"),
        P(),
        P(),
    )
    out_specs = P(None, "ka", None)
    return jax.shard_map(body, mesh=mesh, in_specs=in_specs, out_specs=out_specs, check_vma=False)
```

```python
import math

import jax
import jax.numpy as jnp
import numpy as np
from jax import lax
from jax.experimental import pallas as pl
from jax.experimental.pallas import tpu as pltpu
from jax.sharding import PartitionSpec as P

N1 = 64
NG = 4096
MB = 72
NBD = 8
QSTEPS = 2
KA = 16
GA = 8
F32 = jnp.float32
BF16 = jnp.bfloat16
VMEM_BYTES = 24 * 1024 * 1024
WHOLE_VMEM = 63 * 1024 * 1024
ALL = ("ka", "ga")


def split_table(table):
    high = table.astype(jnp.bfloat16)
    low = (table - high.astype(np.float64)).astype(jnp.bfloat16)
    return high, low


def make_tables():
    places = np.arange(N1)
    angle = (places[:, None] * places[None, :] % N1) * (2.0 * math.pi / N1)
    cos, sin = np.cos(angle), np.sin(angle)
    high, low = split_table(np.concatenate([cos, sin], 0))
    exact_in = np.concatenate([high, low], 1)
    split_in = np.concatenate([high, high, low], 1)
    wide = np.concatenate([cos, sin], 1)
    block = np.zeros((2 * N1, 4 * N1))
    block[:N1, : 2 * N1] = wide
    block[N1:, 2 * N1 :] = wide
    high, low = split_table(block)
    turned = np.concatenate([high, high, low], 0)
    return exact_in, split_in, turned


def lane_sign(rows, first):
    lane = lax.broadcasted_iota(jnp.int32, (rows, 128), 1)
    return jnp.where(lane < 64, first, -first).astype(F32)


def swap_halves(x):
    return pltpu.roll(x, 64, 1)


def split_rows(x):
    high = x.astype(BF16)
    low = (x - high.astype(F32)).astype(BF16)
    return high, low


def dot(a, b):
    return jnp.dot(a, b, preferred_element_type=F32)


def pack_kernel(own_ref, w_hbm, band_hbm, diag_hbm, out_ref, columns_ref, rows_ref, w_ref, band_ref, diag_ref, sems):
    own = own_ref[0]
    band_copy = pltpu.make_async_copy(band_hbm, band_ref, sems.at[0])
    diag_copy = pltpu.make_async_copy(diag_hbm.at[own], diag_ref, sems.at[1])
    band_copy.start()
    diag_copy.start()
    w_copies = []
    for block in range(4):
        lines = pl.ds(block * 128, 128)
        copy = pltpu.make_async_copy(w_hbm.at[:, :, lines], w_ref.at[:, :, lines], sems.at[2 + block])
        copy.start()
        w_copies.append(copy)
    band_copy.wait()
    diag_copy.wait()
    rows_ref[16:24, :] = jnp.zeros((8, NG), F32)
    for band in range(8):
        rows_ref[band : band + 1, :] = band_ref[band, 0:1, :]
        rows_ref[8 + band : 9 + band, :] = band_ref[band, 1:2, :]
    rows_ref[16:18, :] = band_ref[8]
    diag = diag_ref[...]
    high = diag.astype(BF16).astype(F32)
    rows_ref[18:20, :] = high
    rows_ref[20:22, :] = diag - high
    for pair in range(16):
        lanes = [slice((pair * 2 + side) * 128, (pair * 2 + side + 1) * 128) for side in range(2)]
        block = jnp.concatenate([rows_ref[:, lane] for lane in lanes], 0).astype(BF16)
        columns_ref[2 * pair] = block
        columns_ref[2 * pair + 1] = block
        first = 512 + pair % 2 * 48
        out_ref[pair // 2, first : first + 48, :] = block
    lane = lax.broadcasted_iota(jnp.int32, (128, 128), 1) // 32
    for block in range(4):
        w_copies[block].wait()
        lines = slice(block * 128, (block + 1) * 128)
        for dest in range(GA):
            half, place = dest // 4, dest % 4
            total = None
            for slot in range(4):
                part, qstep = slot // 2, slot % 2
                source = w_ref[qstep, part, lines, half * 128 : (half + 1) * 128]
                shift = (slot - place) * 32 % 128
                moved = pltpu.roll(source, shift, 1) if shift else source
                total = moved if total is None else jnp.where(lane == slot, moved, total)
            out_ref[dest, lines, :] = total.astype(BF16)


def scatter_rows(place_ref, from_ref, to_ref):
    def step(block, carry):
        for inner in range(256):
            row = block * 256 + inner
            to_ref[pl.ds(place_ref[row], 1), :] = from_ref[pl.ds(row, 1), :]
        return carry

    lax.fori_loop(0, NG // 256, step, 0)


def first_axis(exact_ref, grid_ref, half_ref, sign):
    table = exact_ref[...]
    signs = lane_sign(64, sign)

    def step(pair, carry):
        rows = grid_ref[pl.ds(pl.multiple_of(pair * 128, 128), 128), :].astype(BF16)
        left, right = rows[:64], rows[64:]
        stacked = jnp.concatenate(
            [jnp.concatenate([left, left], 0), jnp.concatenate([right, right], 0)], 1
        )
        out = dot(table, stacked)
        for side in range(2):
            piece = out[:, side * 128 : (side + 1) * 128]
            mixed = piece[:64] + signs * swap_halves(piece[64:])
            half_ref[pl.ds(pl.multiple_of(pair * 128 + side * 64, 64), 64), :] = mixed
        return carry

    lax.fori_loop(0, 32, step, 0, unroll=32)


def rows_kernel(place_ref, got_ref, exact_ref, turned_ref, out_hbm, out_ref, flat_ref, grid_ref, half_ref, sems):
    for source in range(GA):
        flat_ref[source * 512 : (source + 1) * 512, :] = got_ref[source, 0:512, :].astype(F32)
    scatter_rows(place_ref, flat_ref, grid_ref)
    first_axis(exact_ref, grid_ref, half_ref, -1.0)
    signs = lane_sign(64, -1.0)
    table = turned_ref[...]
    sent = []
    for owner in range(GA):
        for duo in range(2):
            first = owner * 8 + duo * 4
            lefts = []
            for pair in range(2):
                both = jnp.concatenate(
                    [half_ref[pl.ds(first + pair * 2 + side, 64, stride=64), :] for side in range(2)], 0
                )
                high, low = split_rows(both.T)
                lefts.append(jnp.concatenate([high, low, high], 1))
            out = dot(jnp.concatenate(lefts, 0), table)
            for place in range(4):
                pair, side = place // 2, place % 2
                piece = out[pair * 128 : (pair + 1) * 128, side * 128 : (side + 1) * 128]
                mixed = (piece[:64] + signs * swap_halves(piece[64:])).astype(BF16)
                for qstep in range(2):
                    out_ref[owner, qstep * 8 + duo * 4 + place] = mixed[qstep * 32 : (qstep + 1) * 32]
        copy = pltpu.make_async_copy(out_ref.at[owner], out_hbm.at[:, owner], sems.at[owner])
        copy.start()
        sent.append(copy)
    for copy in sent:
        copy.wait()


def columns_kernel(place_ref, got_ref, exact_ref, split_ref, out_hbm, out_ref, flat_ref, grid_ref, half_ref, sems):
    def unpack(index, carry):
        flat_ref[pl.ds(pl.multiple_of(index * 32, 32), 32), :] = got_ref[index, 0:32, :].astype(F32)
        return carry

    lax.fori_loop(0, KA * GA, unpack, 0, unroll=16)
    scatter_rows(place_ref, flat_ref, grid_ref)
    first_axis(exact_ref, grid_ref, half_ref, 1.0)
    signs = lane_sign(64, 1.0)
    table = split_ref[...]

    sent = []
    for pair in range(32):
        columns = []
        for side in range(2):
            high, low = split_rows(half_ref[pl.ds(pair * 2 + side, 64, stride=64), :])
            columns.append(jnp.concatenate([high, low, high], 0))
        out = dot(table, jnp.concatenate(columns, 1))
        for side in range(2):
            piece = out[:, side * 128 : (side + 1) * 128]
            mixed = piece[:64] + signs * swap_halves(piece[64:])
            out_ref[pair * 128 + side * 64 : pair * 128 + side * 64 + 64, :] = mixed.astype(BF16)
        if pair % 8 == 7:
            lines = pl.ds((pair - 7) * 128, 1024)
            copy = pltpu.make_async_copy(out_ref.at[lines], out_hbm.at[lines], sems.at[pair // 8])
            copy.start()
            sent.append(copy)
    for copy in sent:
        copy.wait()


def pick_diag(rows):
    line = lax.broadcasted_iota(jnp.int32, (16, 192), 0)
    place = lax.broadcasted_iota(jnp.int32, (16, 192), 1)
    first = line % 8 * 24 + 18 + line // 8
    pick = jnp.where((place == first) | (place == first + 2), 1.0, 0.0).astype(BF16)
    return dot(pick, rows)


def row_side_kernel(own_ref, *refs):
    *part_refs, rows_ref, diag_ref = refs
    own = own_ref[0]
    z_own, x_own, c_own = own // 8, own // 2 % 4, own % 2
    for flip in range(2):
        for shift in range(4):
            for turn in range(2):
                from_ref = part_refs[flip * 4 + shift]
                point = (z_own + turn) % 2 * 8 + (x_own + 4 - shift) % 4 * 2 + (c_own + flip) % 2
                for pair in range(4):
                    blocks = []
                    for source in (2 * pair, 2 * pair + 1):
                        block = from_ref[turn, source].astype(F32)
                        blocks.append(
                            jnp.concatenate([block[24 * group : 24 * group + 24] for group in range(4)], 1)
                        )
                    rows_ref[point, 48 * pair : 48 * pair + 48, :] = jnp.concatenate(blocks, 0).astype(BF16)

    def step(point, carry):
        diag_ref[point] = pick_diag(rows_ref[point])
        return carry

    lax.fori_loop(0, KA, step, 0, unroll=4)


def column_side_kernel(own_ref, *refs):
    *part_refs, turned_ref, left_ref, whole_ref = refs
    y_own = own_ref[0] // 2
    for shift in range(4):
        whole_ref[(y_own + 4 - shift) % 4] = part_refs[shift][...]
    line = lax.broadcasted_iota(jnp.int32, (8, 256), 0)

    def step(point, carry):
        plain, straight, crossed = [], [], []
        for source in range(GA):
            block = whole_ref[source // 2, 2 * point + source % 2].astype(F32)
            block = jnp.concatenate([block[:24], block[24:]], 1)
            plain.append(block)
            real, imag, rest = block[:8], block[8:16], block[16:]
            straight += [real, imag, jnp.where(line < 2, rest, 0.0)]
            swapped = jnp.where(line == 0, pltpu.roll(rest, 7, 0), -pltpu.roll(rest, 1, 0))
            crossed += [imag, -real, jnp.where(line < 2, swapped, 0.0)]
        diag = pick_diag(jnp.concatenate(plain, 0).astype(BF16))
        diag_re, diag_im = diag[:8], diag[8:]
        both = jnp.concatenate(
            [jnp.concatenate([diag_re, diag_im], 1), jnp.concatenate([-diag_im, diag_re], 1)], 0
        )
        high, low = split_rows(both)
        left_ref[point] = jnp.concatenate([high, low], 0)
        turned_ref[point, 0:256, :] = jnp.concatenate(straight, 0).T.astype(BF16)
        turned_ref[point, 256:512, :] = jnp.concatenate(crossed, 0).T.astype(BF16)
        return carry

    lax.fori_loop(0, KA, step, 0, unroll=2)


def fill_tiles(screen_ref, tile_ref):
    lane = lax.broadcasted_iota(jnp.int32, (256, 128), 1) < 64
    for qstep in range(2):
        for group in range(4):
            even = screen_ref[qstep * 8 + group * 2].astype(F32)
            odd = screen_ref[qstep * 8 + group * 2 + 1].astype(F32)
            lanes = slice(group % 2 * 128, (group % 2 + 1) * 128)
            tile_ref[qstep, 0, group // 2, :, lanes] = jnp.where(lane, even, swap_halves(odd))
            tile_ref[qstep, 1, group // 2, :, lanes] = jnp.where(lane, swap_halves(even), odd)


def contract_kernel(point_ref, screen_ref, row_ref, far_ref, turned_ref, left_ref, out_ref, sum_ref, tile_ref):
    first = pl.program_id(0) * 4

    @pl.when(first == 0)
    def _():
        sum_ref[...] = jnp.zeros_like(sum_ref)
        fill_tiles(screen_ref, tile_ref)

    for inner in range(4):
        turned = turned_ref[inner]
        for half in range(2):
            lanes = slice(half * 256, (half + 1) * 256)
            product = dot(turned, row_ref[inner, :, lanes])
            real, imag = product[:256], product[256:]
            for qstep in range(2):
                point = point_ref[qstep, first + inner]
                screen_re, screen_im = tile_ref[qstep, 0, half], tile_ref[qstep, 1, half]
                mixed_re = (screen_re * real - screen_im * imag).astype(BF16)
                mixed_im = (screen_re * imag + screen_im * real).astype(BF16)
                total = dot(left_ref[point], jnp.concatenate([mixed_re, mixed_im], 0))
                total = total[:16] + total[16:]
                far = far_ref[point, :, lanes]
                far_re, far_im = far[:8], far[8:]
                total_re, total_im = total[:8], total[8:]
                sum_re = far_re * total_re - far_im * total_im
                sum_im = far_re * total_im + far_im * total_re
                both = jnp.concatenate([sum_re, sum_im], 0)
                sum_ref[point] += both[:, :128] + both[:, 128:]

    @pl.when(first == KA - 4)
    def _():
        value = jnp.sum(sum_ref[...], axis=2)
        out_ref[...] = jnp.broadcast_to(value[:, None, :], (KA, GA, 16))


def call(kernel, outs, scratch, smem, *operands, space=pltpu.VMEM, limit=VMEM_BYTES, far_outs=0):
    smem_spec = [pl.BlockSpec(memory_space=pltpu.SMEM)] * smem
    vmem_spec = [pl.BlockSpec(memory_space=space)] * (len(operands) - smem)
    return pl.pallas_call(
        kernel,
        out_shape=[jax.ShapeDtypeStruct(shape, kind) for shape, kind in outs],
        in_specs=smem_spec + vmem_spec,
        out_specs=[
            pl.BlockSpec(memory_space=pl.ANY if index < far_outs else pltpu.VMEM) for index in range(len(outs))
        ],
        scratch_shapes=scratch,
        compiler_params=pltpu.CompilerParams(vmem_limit_bytes=limit),
    )(*operands)


def flip_z(part):
    return lax.ppermute(part, "ka", [(index, index ^ 8) for index in range(KA)])


def along_x(part, shift):
    return lax.ppermute(part, "ka", [(index, index // 8 * 8 + (index + 2 * shift) % 8) for index in range(KA)])


def along_y(part):
    parts = [part]
    for shift in range(1, 4):
        along = [(index, (index + 2 * shift) % GA) for index in range(GA)]
        parts.append(lax.ppermute(part, "ga", along))
    return parts


def flip_core(part):
    return lax.ppermute(part, "ka", [(index, index ^ 1) for index in range(KA)])


def body(diag_waves, band_waves, screening, partner_map, grid_index):
    own_k = lax.axis_index("ka").astype(jnp.int32).reshape(1)
    own_g = lax.axis_index("ga").astype(jnp.int32).reshape(1)
    exact_in, split_in, turned = [jnp.asarray(table) for table in make_tables()]
    place = (grid_index % N1) * N1 + grid_index // N1
    points = jnp.arange(KA, dtype=jnp.int32)
    owners = jnp.sum(
        jnp.where(partner_map[:, :, None] == points[None, None, :], points[None, :, None], 0), axis=1
    )
    work = [pltpu.VMEM((NG, 128), F32)] * 3
    packed, columns = call(
        pack_kernel,
        [((GA, 608, 128), BF16), ((2 * KA, 48, 128), BF16)],
        [
            pltpu.VMEM((24, NG), F32),
            pltpu.VMEM((2, 2, 512, 256), F32),
            pltpu.VMEM((9, 2, NG), F32),
            pltpu.VMEM((2, NG), F32),
            pltpu.SemaphoreType.DMA((6,)),
        ],
        1,
        own_g, screening, band_waves[0], diag_waves[0],
        space=pltpu.HBM,
        limit=WHOLE_VMEM,
    )
    packed = lax.all_to_all(packed, "ga", 0, 0)
    packed, columns = lax.optimization_barrier((packed, columns))
    planes = [[ka * GA + 2 * y + z for ka in range(KA) for z in range(2)] for y in range(4)]
    columns = lax.all_to_all(columns, ALL, 0, 0, axis_index_groups=planes)
    own_part = packed[:, 512:608]
    flipped_part = flip_z(own_part)
    (spread,) = call(
        rows_kernel,
        [((KA, GA, 32, 128), BF16)],
        [pltpu.VMEM((GA, KA, 32, 128), BF16), *work, pltpu.SemaphoreType.DMA((GA,))],
        1,
        place, packed, exact_in, turned,
        far_outs=1,
    )
    spread = spread.reshape(KA * GA, 32, 128)
    spread, flipped_part, columns = lax.optimization_barrier((spread, flipped_part, columns))
    own_part = jnp.stack([own_part, flipped_part])
    parts = [along_x(own_part, 1), along_x(own_part, 3)]
    column_parts = along_y(columns)
    spread = lax.all_to_all(spread, ALL, 0, 0)
    spread, far_part = lax.optimization_barrier((spread, own_part))
    far_part = along_x(far_part, 2)
    (screen,) = call(
        columns_kernel,
        [((NG, 128), BF16)],
        [pltpu.VMEM((NG, 128), BF16), *work, pltpu.SemaphoreType.DMA((4,))],
        1,
        place, spread, exact_in, split_in,
        far_outs=1,
    )
    parts, column_parts, far_part, screen = lax.optimization_barrier((parts, column_parts, far_part, screen))
    screen = lax.all_to_all(screen.reshape(KA, 256, 128), "ka", 0, 0)
    parts = [own_part, parts[0], far_part, parts[1]]
    parts += [flip_core(part) for part in parts]
    rows, far = call(
        row_side_kernel, [((KA, 192, 512), BF16), ((KA, 16, 512), F32)], [], 1, own_k, *parts
    )
    near, left = call(
        column_side_kernel, [((KA, 512, 192), BF16), ((KA, 32, 512), BF16)],
        [pltpu.VMEM((4, 2 * KA, 48, 128), BF16)],
        1,
        own_g, *column_parts,
    )
    partial = pl.pallas_call(
        contract_kernel,
        out_shape=jax.ShapeDtypeStruct((KA, GA, 16), F32),
        grid=(4,),
        in_specs=[
            pl.BlockSpec(memory_space=pltpu.SMEM),
            pl.BlockSpec((KA, 256, 128), lambda step: (0, 0, 0)),
            pl.BlockSpec((4, 192, 512), lambda step: (step, 0, 0)),
            pl.BlockSpec((KA, 16, 512), lambda step: (0, 0, 0)),
            pl.BlockSpec((4, 512, 192), lambda step: (step, 0, 0)),
            pl.BlockSpec((KA, 32, 512), lambda step: (0, 0, 0)),
        ],
        out_specs=pl.BlockSpec((KA, GA, 16), lambda step: (0, 0, 0)),
        scratch_shapes=[pltpu.VMEM((KA, 16, 128), F32), pltpu.VMEM((2, 2, 2, 256, 256), F32)],
        compiler_params=pltpu.CompilerParams(vmem_limit_bytes=WHOLE_VMEM),
    )(owners, screen, rows, far, near, left)
    value = partial.reshape(KA * GA, 16)
    value = jnp.sum(lax.all_to_all(value, ALL, 0, 0, tiled=True), axis=0)
    return value.reshape(2, 1, NBD) * (-1.0 / (QSTEPS * MB * math.sqrt(NG) * NG))


def solution(mesh):
    in_specs = (
        P("ka", None, None, None),
        P("ka", "ga", None, None),
        P(None, None, "ga", "ka"),
        P(),
        P(),
    )
    out_specs = P(None, "ka", None)
    return jax.shard_map(body, mesh=mesh, in_specs=in_specs, out_specs=out_specs, check_vma=False)
```

```python
import math

import jax
import jax.numpy as jnp
import numpy as np
from jax import lax
from jax.experimental import pallas as pl
from jax.experimental.pallas import tpu as pltpu
from jax.sharding import PartitionSpec as P

N1 = 64
NG = 4096
MB = 72
NBD = 8
QSTEPS = 2
KA = 16
GA = 8
F32 = jnp.float32
BF16 = jnp.bfloat16
VMEM_BYTES = 24 * 1024 * 1024
WHOLE_VMEM = 63 * 1024 * 1024
ALL = ("ka", "ga")


def split_table(table):
    high = table.astype(jnp.bfloat16)
    low = (table - high.astype(np.float64)).astype(jnp.bfloat16)
    return high, low


def make_tables():
    places = np.arange(N1)
    angle = (places[:, None] * places[None, :] % N1) * (2.0 * math.pi / N1)
    cos, sin = np.cos(angle), np.sin(angle)
    high, low = split_table(np.concatenate([cos, sin], 0))
    exact_in = np.concatenate([high, low], 1)
    split_in = np.concatenate([high, high, low], 1)
    wide = np.concatenate([cos, sin], 1)
    block = np.zeros((2 * N1, 4 * N1))
    block[:N1, : 2 * N1] = wide
    block[N1:, 2 * N1 :] = wide
    high, low = split_table(block)
    turned = np.concatenate([high, high, low], 0)
    return exact_in, split_in, turned


def lane_sign(rows, first):
    lane = lax.broadcasted_iota(jnp.int32, (rows, 128), 1)
    return jnp.where(lane < 64, first, -first).astype(F32)


def swap_halves(x):
    return pltpu.roll(x, 64, 1)


def split_rows(x):
    high = x.astype(BF16)
    low = (x - high.astype(F32)).astype(BF16)
    return high, low


def dot(a, b):
    return jnp.dot(a, b, preferred_element_type=F32)


def pack_kernel(own_ref, w_hbm, band_hbm, diag_hbm, out_ref, columns_ref, rows_ref, w_ref, band_ref, diag_ref, sems):
    own = own_ref[0]
    band_copy = pltpu.make_async_copy(band_hbm, band_ref, sems.at[0])
    diag_copy = pltpu.make_async_copy(diag_hbm.at[own], diag_ref, sems.at[1])
    band_copy.start()
    diag_copy.start()
    w_copies = []
    for block in range(4):
        lines = pl.ds(block * 128, 128)
        copy = pltpu.make_async_copy(w_hbm.at[:, :, lines], w_ref.at[:, :, lines], sems.at[2 + block])
        copy.start()
        w_copies.append(copy)
    band_copy.wait()
    diag_copy.wait()
    rows_ref[16:24, :] = jnp.zeros((8, NG), F32)
    for band in range(8):
        rows_ref[band : band + 1, :] = band_ref[band, 0:1, :]
        rows_ref[8 + band : 9 + band, :] = band_ref[band, 1:2, :]
    rows_ref[16:18, :] = band_ref[8]
    diag = diag_ref[...]
    high = diag.astype(BF16).astype(F32)
    rows_ref[18:20, :] = high
    rows_ref[20:22, :] = diag - high
    for pair in range(16):
        lanes = [slice((pair * 2 + side) * 128, (pair * 2 + side + 1) * 128) for side in range(2)]
        block = jnp.concatenate([rows_ref[:, lane] for lane in lanes], 0).astype(BF16)
        columns_ref[2 * pair] = block
        columns_ref[2 * pair + 1] = block
        first = 512 + pair % 2 * 48
        out_ref[pair // 2, first : first + 48, :] = block
    lane = lax.broadcasted_iota(jnp.int32, (128, 128), 1) // 32
    for block in range(4):
        w_copies[block].wait()
        lines = slice(block * 128, (block + 1) * 128)
        for dest in range(GA):
            half, place = dest // 4, dest % 4
            total = None
            for slot in range(4):
                part, qstep = slot // 2, slot % 2
                source = w_ref[qstep, part, lines, half * 128 : (half + 1) * 128]
                shift = (slot - place) * 32 % 128
                moved = pltpu.roll(source, shift, 1) if shift else source
                total = moved if total is None else jnp.where(lane == slot, moved, total)
            out_ref[dest, lines, :] = total.astype(BF16)


def scatter_rows(place_ref, from_ref, to_ref):
    def step(block, carry):
        for inner in range(256):
            row = block * 256 + inner
            to_ref[pl.ds(place_ref[row], 1), :] = from_ref[pl.ds(row, 1), :]
        return carry

    lax.fori_loop(0, NG // 256, step, 0)


def first_axis(exact_ref, grid_ref, half_ref, sign):
    table = exact_ref[...]
    signs = lane_sign(64, sign)

    def step(pair, carry):
        rows = grid_ref[pl.ds(pl.multiple_of(pair * 128, 128), 128), :].astype(BF16)
        left, right = rows[:64], rows[64:]
        stacked = jnp.concatenate(
            [jnp.concatenate([left, left], 0), jnp.concatenate([right, right], 0)], 1
        )
        out = dot(table, stacked)
        for side in range(2):
            piece = out[:, side * 128 : (side + 1) * 128]
            mixed = piece[:64] + signs * swap_halves(piece[64:])
            half_ref[pl.ds(pl.multiple_of(pair * 128 + side * 64, 64), 64), :] = mixed
        return carry

    lax.fori_loop(0, 32, step, 0, unroll=32)


def rows_kernel(place_ref, got_ref, exact_ref, turned_ref, out_hbm, out_ref, flat_ref, grid_ref, half_ref, sems):
    for source in range(GA):
        flat_ref[source * 512 : (source + 1) * 512, :] = got_ref[source, 0:512, :].astype(F32)
    scatter_rows(place_ref, flat_ref, grid_ref)
    first_axis(exact_ref, grid_ref, half_ref, -1.0)
    signs = lane_sign(64, -1.0)
    table = turned_ref[...]
    sent = []
    for owner in range(GA):
        for duo in range(2):
            first = owner * 8 + duo * 4
            lefts = []
            for pair in range(2):
                both = jnp.concatenate(
                    [half_ref[pl.ds(first + pair * 2 + side, 64, stride=64), :] for side in range(2)], 0
                )
                high, low = split_rows(both.T)
                lefts.append(jnp.concatenate([high, low, high], 1))
            out = dot(jnp.concatenate(lefts, 0), table)
            for place in range(4):
                pair, side = place // 2, place % 2
                piece = out[pair * 128 : (pair + 1) * 128, side * 128 : (side + 1) * 128]
                mixed = (piece[:64] + signs * swap_halves(piece[64:])).astype(BF16)
                for qstep in range(2):
                    out_ref[owner, qstep * 8 + duo * 4 + place] = mixed[qstep * 32 : (qstep + 1) * 32]
        copy = pltpu.make_async_copy(out_ref.at[owner], out_hbm.at[:, owner], sems.at[owner])
        copy.start()
        sent.append(copy)
    for copy in sent:
        copy.wait()


def columns_kernel(place_ref, got_ref, exact_ref, split_ref, out_hbm, out_ref, flat_ref, grid_ref, half_ref, sems):
    def unpack(index, carry):
        flat_ref[pl.ds(pl.multiple_of(index * 32, 32), 32), :] = got_ref[index, 0:32, :].astype(F32)
        return carry

    lax.fori_loop(0, KA * GA, unpack, 0, unroll=16)
    scatter_rows(place_ref, flat_ref, grid_ref)
    first_axis(exact_ref, grid_ref, half_ref, 1.0)
    signs = lane_sign(64, 1.0)
    table = split_ref[...]

    sent = []
    for pair in range(32):
        columns = []
        for side in range(2):
            high, low = split_rows(half_ref[pl.ds(pair * 2 + side, 64, stride=64), :])
            columns.append(jnp.concatenate([high, low, high], 0))
        out = dot(table, jnp.concatenate(columns, 1))
        for side in range(2):
            piece = out[:, side * 128 : (side + 1) * 128]
            mixed = piece[:64] + signs * swap_halves(piece[64:])
            out_ref[pair * 128 + side * 64 : pair * 128 + side * 64 + 64, :] = mixed.astype(BF16)
        if pair % 8 == 7:
            lines = pl.ds((pair - 7) * 128, 1024)
            copy = pltpu.make_async_copy(out_ref.at[lines], out_hbm.at[lines], sems.at[pair // 8])
            copy.start()
            sent.append(copy)
    for copy in sent:
        copy.wait()


def pick_diag(rows):
    line = lax.broadcasted_iota(jnp.int32, (16, 192), 0)
    place = lax.broadcasted_iota(jnp.int32, (16, 192), 1)
    first = line % 8 * 24 + 18 + line // 8
    pick = jnp.where((place == first) | (place == first + 2), 1.0, 0.0).astype(BF16)
    return dot(pick, rows)


def row_side_kernel(own_ref, *refs):
    *part_refs, rows_ref, diag_ref = refs
    own = own_ref[0]
    z_own, x_own, c_own = own // 8, own // 2 % 4, own % 2
    for flip in range(2):
        for shift in range(4):
            for turn in range(2):
                own_pair, up, down, *far = part_refs[flip * 5 : flip * 5 + 5]
                from_ref = (own_pair, up, far[turn], down)[shift]
                point = (z_own + turn) % 2 * 8 + (x_own + 4 - shift) % 4 * 2 + (c_own + flip) % 2
                for pair in range(4):
                    blocks = []
                    for source in (2 * pair, 2 * pair + 1):
                        block = (from_ref[source] if shift == 2 else from_ref[turn, source]).astype(F32)
                        blocks.append(
                            jnp.concatenate([block[24 * group : 24 * group + 24] for group in range(4)], 1)
                        )
                    rows_ref[point, 48 * pair : 48 * pair + 48, :] = jnp.concatenate(blocks, 0).astype(BF16)

    def step(point, carry):
        diag_ref[point] = pick_diag(rows_ref[point])
        return carry

    lax.fori_loop(0, KA, step, 0, unroll=4)


def column_side_kernel(own_ref, *refs):
    *part_refs, turned_ref, left_ref, whole_ref = refs
    y_own = own_ref[0] // 2
    for shift in range(4):
        whole_ref[(y_own + 4 - shift) % 4] = part_refs[shift][...]
    line = lax.broadcasted_iota(jnp.int32, (8, 256), 0)

    def step(point, carry):
        plain, straight, crossed = [], [], []
        for source in range(GA):
            block = whole_ref[source // 2, 2 * point + source % 2].astype(F32)
            block = jnp.concatenate([block[:24], block[24:]], 1)
            plain.append(block)
            real, imag, rest = block[:8], block[8:16], block[16:]
            straight += [real, imag, jnp.where(line < 2, rest, 0.0)]
            swapped = jnp.where(line == 0, pltpu.roll(rest, 7, 0), -pltpu.roll(rest, 1, 0))
            crossed += [imag, -real, jnp.where(line < 2, swapped, 0.0)]
        diag = pick_diag(jnp.concatenate(plain, 0).astype(BF16))
        diag_re, diag_im = diag[:8], diag[8:]
        both = jnp.concatenate(
            [jnp.concatenate([diag_re, diag_im], 1), jnp.concatenate([-diag_im, diag_re], 1)], 0
        )
        high, low = split_rows(both)
        left_ref[point] = jnp.concatenate([high, low], 0)
        turned_ref[point, 0:256, :] = jnp.concatenate(straight, 0).T.astype(BF16)
        turned_ref[point, 256:512, :] = jnp.concatenate(crossed, 0).T.astype(BF16)
        return carry

    lax.fori_loop(0, KA, step, 0, unroll=2)


def fill_tiles(screen_ref, tile_ref):
    lane = lax.broadcasted_iota(jnp.int32, (256, 128), 1) < 64
    for qstep in range(2):
        for group in range(4):
            even = screen_ref[qstep * 8 + group * 2].astype(F32)
            odd = screen_ref[qstep * 8 + group * 2 + 1].astype(F32)
            lanes = slice(group % 2 * 128, (group % 2 + 1) * 128)
            tile_ref[qstep, 0, group // 2, :, lanes] = jnp.where(lane, even, swap_halves(odd))
            tile_ref[qstep, 1, group // 2, :, lanes] = jnp.where(lane, swap_halves(even), odd)


def contract_kernel(point_ref, screen_ref, row_ref, far_ref, turned_ref, left_ref, out_ref, sum_ref, tile_ref):
    first = pl.program_id(0) * 4

    @pl.when(first == 0)
    def _():
        sum_ref[...] = jnp.zeros_like(sum_ref)
        fill_tiles(screen_ref, tile_ref)

    for inner in range(4):
        turned = turned_ref[inner]
        for half in range(2):
            lanes = slice(half * 256, (half + 1) * 256)
            product = dot(turned, row_ref[inner, :, lanes])
            real, imag = product[:256], product[256:]
            for qstep in range(2):
                point = point_ref[qstep, first + inner]
                screen_re, screen_im = tile_ref[qstep, 0, half], tile_ref[qstep, 1, half]
                mixed_re = (screen_re * real - screen_im * imag).astype(BF16)
                mixed_im = (screen_re * imag + screen_im * real).astype(BF16)
                total = dot(left_ref[point], jnp.concatenate([mixed_re, mixed_im], 0))
                total = total[:16] + total[16:]
                far = far_ref[point, :, lanes]
                far_re, far_im = far[:8], far[8:]
                total_re, total_im = total[:8], total[8:]
                sum_re = far_re * total_re - far_im * total_im
                sum_im = far_re * total_im + far_im * total_re
                both = jnp.concatenate([sum_re, sum_im], 0)
                sum_ref[point] += both[:, :128] + both[:, 128:]

    @pl.when(first == KA - 4)
    def _():
        value = jnp.sum(sum_ref[...], axis=2)
        value = value * (-1.0 / (QSTEPS * MB * math.sqrt(NG) * NG))
        out_ref[...] = jnp.broadcast_to(value[:, None, :], (KA, GA, 16))


def call(kernel, outs, scratch, smem, *operands, space=pltpu.VMEM, limit=VMEM_BYTES, far_outs=0):
    smem_spec = [pl.BlockSpec(memory_space=pltpu.SMEM)] * smem
    vmem_spec = [pl.BlockSpec(memory_space=space)] * (len(operands) - smem)
    return pl.pallas_call(
        kernel,
        out_shape=[jax.ShapeDtypeStruct(shape, kind) for shape, kind in outs],
        in_specs=smem_spec + vmem_spec,
        out_specs=[
            pl.BlockSpec(memory_space=pl.ANY if index < far_outs else pltpu.VMEM) for index in range(len(outs))
        ],
        scratch_shapes=scratch,
        compiler_params=pltpu.CompilerParams(vmem_limit_bytes=limit),
    )(*operands)


def flip_z(part):
    return lax.ppermute(part, "ka", [(index, index ^ 8) for index in range(KA)])


def along_x(part, shift):
    return lax.ppermute(part, "ka", [(index, index // 8 * 8 + (index + 2 * shift) % 8) for index in range(KA)])


def along_y(part):
    parts = [part]
    for shift in range(1, 4):
        along = [(index, (index + 2 * shift) % GA) for index in range(GA)]
        parts.append(lax.ppermute(part, "ga", along))
    return parts


def flip_core(part):
    return lax.ppermute(part, "ka", [(index, index ^ 1) for index in range(KA)])


def body(diag_waves, band_waves, screening, partner_map, grid_index):
    own_k = lax.axis_index("ka").astype(jnp.int32).reshape(1)
    own_g = lax.axis_index("ga").astype(jnp.int32).reshape(1)
    exact_in, split_in, turned = [jnp.asarray(table) for table in make_tables()]
    place = (grid_index % N1) * N1 + grid_index // N1
    points = jnp.arange(KA, dtype=jnp.int32)
    owners = jnp.sum(
        jnp.where(partner_map[:, :, None] == points[None, None, :], points[None, :, None], 0), axis=1
    )
    work = [pltpu.VMEM((NG, 128), F32)] * 3
    packed, columns = call(
        pack_kernel,
        [((GA, 608, 128), BF16), ((2 * KA, 48, 128), BF16)],
        [
            pltpu.VMEM((24, NG), F32),
            pltpu.VMEM((2, 2, 512, 256), F32),
            pltpu.VMEM((9, 2, NG), F32),
            pltpu.VMEM((2, NG), F32),
            pltpu.SemaphoreType.DMA((6,)),
        ],
        1,
        own_g, screening, band_waves[0], diag_waves[0],
        space=pltpu.HBM,
        limit=WHOLE_VMEM,
    )
    packed = lax.all_to_all(packed, "ga", 0, 0)
    packed, columns = lax.optimization_barrier((packed, columns))
    planes = [[ka * GA + 2 * y + z for ka in range(KA) for z in range(2)] for y in range(4)]
    columns = lax.all_to_all(columns, ALL, 0, 0, axis_index_groups=planes)
    own_part = packed[:, 512:608]
    flipped_part = flip_z(own_part)
    far_part = along_x(own_part, 2)
    (spread,) = call(
        rows_kernel,
        [((KA, GA, 32, 128), BF16)],
        [pltpu.VMEM((GA, KA, 32, 128), BF16), *work, pltpu.SemaphoreType.DMA((GA,))],
        1,
        place, packed, exact_in, turned,
        far_outs=1,
    )
    spread = spread.reshape(KA * GA, 32, 128)
    spread, flipped_part, far_part, columns = lax.optimization_barrier((spread, flipped_part, far_part, columns))
    own_part = jnp.stack([own_part, flipped_part])
    parts = [along_x(own_part, 1), along_x(own_part, 3)]
    column_parts = along_y(columns)
    spread = lax.all_to_all(spread, ALL, 0, 0)
    far_parts = [far_part, flip_z(far_part)]
    spread, columns = lax.optimization_barrier((spread, columns))
    column_parts[2] = along_y(columns)[2]
    (screen,) = call(
        columns_kernel,
        [((NG, 128), BF16)],
        [pltpu.VMEM((NG, 128), BF16), *work, pltpu.SemaphoreType.DMA((4,))],
        1,
        place, spread, exact_in, split_in,
        far_outs=1,
    )
    parts, column_parts, far_parts, screen = lax.optimization_barrier((parts, column_parts, far_parts, screen))
    screen = lax.all_to_all(screen.reshape(KA, 256, 128), "ka", 0, 0)
    parts = [own_part, *parts, *far_parts]
    parts += [flip_core(part) for part in parts]
    rows, far = call(
        row_side_kernel, [((KA, 192, 512), BF16), ((KA, 16, 512), F32)], [], 1, own_k, *parts
    )
    near, left = call(
        column_side_kernel, [((KA, 512, 192), BF16), ((KA, 32, 512), BF16)],
        [pltpu.VMEM((4, 2 * KA, 48, 128), BF16)],
        1,
        own_g, *column_parts,
    )
    partial = pl.pallas_call(
        contract_kernel,
        out_shape=jax.ShapeDtypeStruct((KA, GA, 16), F32),
        grid=(4,),
        in_specs=[
            pl.BlockSpec(memory_space=pltpu.SMEM),
            pl.BlockSpec((KA, 256, 128), lambda step: (0, 0, 0)),
            pl.BlockSpec((4, 192, 512), lambda step: (step, 0, 0)),
            pl.BlockSpec((KA, 16, 512), lambda step: (0, 0, 0)),
            pl.BlockSpec((4, 512, 192), lambda step: (step, 0, 0)),
            pl.BlockSpec((KA, 32, 512), lambda step: (0, 0, 0)),
        ],
        out_specs=pl.BlockSpec((KA, GA, 16), lambda step: (0, 0, 0)),
        scratch_shapes=[pltpu.VMEM((KA, 16, 128), F32), pltpu.VMEM((2, 2, 2, 256, 256), F32)],
        compiler_params=pltpu.CompilerParams(vmem_limit_bytes=WHOLE_VMEM),
    )(owners, screen, rows, far, near, left)
    value = partial.reshape(KA * GA, 16)
    value = lax.all_to_all(value, ALL, 0, 0, tiled=True).reshape(KA * GA, 2, 1, NBD)
    return jnp.sum(value, axis=0)


def solution(mesh):
    in_specs = (
        P("ka", None, None, None),
        P("ka", "ga", None, None),
        P(None, None, "ga", "ka"),
        P(),
        P(),
    )
    out_specs = P(None, "ka", None)
    return jax.shard_map(body, mesh=mesh, in_specs=in_specs, out_specs=out_specs, check_vma=False)
```
